32 devices in a mesh: dom: 8 (over z, core), head: 4 (over y, x).
Axes of the slice: x: 2, y: 2, z: 4, core: 2. Of those that a mesh axis runs over, the one named last changes fastest.
Arguments:
- features: bfloat16 [16384, 512], P(('dom', 'head')), may hold values from -16 to 16
- tile_pattern: int32 [128, 6, 128, 128], P(('dom', 'head')), may hold values 0 or 1
- tile_source: int32 [128, 6], P(('dom', 'head')), may hold values from 0 to 11
- serve_list: int32 [8, 4, 8, 1], P('dom', 'head'), may hold values from 0 to 3
- key_blocks: int32 [128, 2], P('dom'), may hold values from 0 to 15, all different within a row
- qkv_weight: bfloat16 [512, 1536], replicated, may hold values from -0.25 to 0.25
- attn_weight: bfloat16 [512, 512], replicated, may hold values from -0.25 to 0.25
- norm_gain: float32 [512], replicated, may hold values from 0.5 to 1.5
- expand_weight: bfloat16 [2048, 512], P('head'), may hold values from -0.25 to 0.25
- reduce_weight: bfloat16 [2048, 512], P('head'), may hold values from -0.125 to 0.125
Outputs:
- output: bfloat16 [16384, 512], P(('dom', 'head'))
The draws below stay inside these ranges and needn't reach their ends.
Inputs may be any that keep to these rules, and one draw needn't show every extreme that they name: `key_blocks`: the 2 entries of a row are distinct.
All inputs are finite; a program needn't handle non-finite values. No bound on the sum of `tile_pattern` on one device may be relied on, other than what follows from the above.
Results may differ from the reference program's by a relative error of at most 0.01.
The reference program's roundings to bfloat16 on the way (of `aggregated`, `qkv`, `probabilities`, `context`, `normed` and `hidden`) count: a program that leaves them out, or rounds other values in their place, can miss the bound.
Values may be sent and summed in bfloat16 or wider, within the bound.
A program may use at most 128 MiB of HBM per device.

```python
import jax
import jax.numpy as jnp
from jax import lax

D = 512
HEADS = 16
FF = 2048
HDIM = 32
BLOCK = 128
TPB = 6
SLOTS = 1
BLK_DEV = 4
BLK_PART = 16
KB = 2
NBLK = 128
NODES = 16384
N_DOM = 8
N_HEAD = 4


def draw_features(key, part):
    key_base = jax.random.fold_in(jax.random.fold_in(key, 11), 0)
    values = jax.random.normal(key_base, (NODES, D), jnp.float32)
    return jnp.clip(values, -16.0, 16.0).astype(jnp.bfloat16)


def place_ends(drawn, key, low, largest):
    place = [jax.random.randint(jax.random.fold_in(key, axis), (), 0, length) for axis, length in enumerate(drawn.shape)]
    main_axis = drawn.shape.index(max(drawn.shape))
    neighbour = place[:main_axis] + [(place[main_axis] + 1) % drawn.shape[main_axis]] + place[main_axis + 1:]
    return drawn.at[tuple(place)].set(low).at[tuple(neighbour)].set(largest)


def block_levels(own_key, extent, pieces, least, high):
    def one(dim, shards_of):
        steps = jax.random.uniform(jax.random.fold_in(jax.random.fold_in(own_key, 6), dim), (shards_of,), jnp.float32, least / len(pieces), high / len(pieces))
        return jnp.repeat(jnp.exp(steps), extent[dim] // shards_of).reshape((-1,) + (1,) * (len(extent) - dim - 1))

    gain = one(*pieces[0])
    for cut in pieces[1:]:
        gain = gain * one(*cut)
    return gain


def different_ones(key, rows, count, top, lift):
    ranking = jax.random.permutation(jax.random.fold_in(key, 1), count)
    favour = ranking
    for power in range(3):
        favour = favour * favour // count
    favour = favour * lift // count
    lots = jax.random.randint(jax.random.fold_in(key, 2), (rows, count), 0, 4096) + favour
    fixed_rows = jax.random.permutation(jax.random.fold_in(key, 3), rows)[jnp.arange(count) % rows]
    lots = jnp.where(jnp.arange(rows)[:, None] == fixed_rows[None, :], 1 << 14, lots)
    merit = lots * count + jnp.arange(count)
    return lax.top_k(merit.astype(jnp.int32), top)[1].astype(jnp.int32)


def noise(own_key, shape, deviation, bound, cuts=(), held_as=jnp.bfloat16):
    level = block_levels(own_key, shape, cuts, -0.22, 0.18) if cuts else 1.0
    array = jax.random.normal(own_key, shape, jnp.float32) * deviation * level
    return jnp.minimum(jnp.maximum(array, -bound), bound).astype(held_as)


def setup_inputs(seed: int = 0) -> dict:
    seeds = jax.random.split(jax.random.key(seed), 11)
    features = draw_features(jax.random.fold_in(seeds[10], 71), 0)
    tile_pattern = place_ends((jax.random.randint(seeds[1], (NBLK, TPB, BLOCK, BLOCK), 0, 4) < 1).astype(jnp.int32), jax.random.fold_in(seeds[1], 1), 0, 1)
    tile_source = place_ends(jax.random.randint(seeds[2], (NBLK, TPB), 0, BLK_DEV + N_DOM * SLOTS), jax.random.fold_in(seeds[2], 1), 0, (BLK_DEV + N_DOM * SLOTS) - 1).astype(jnp.int32)
    serve_list = place_ends(jax.random.randint(seeds[3], (N_DOM, N_HEAD, N_DOM, SLOTS), 0, BLK_DEV), jax.random.fold_in(seeds[3], 1), 0, BLK_DEV - 1).astype(jnp.int32)
    key_blocks = different_ones(seeds[4], NBLK, BLK_PART, KB, 0)
    qkv_weight = noise(seeds[5], (D, 3 * D), D ** -0.5, 0.25)
    attn_weight = noise(seeds[6], (D, D), D ** -0.5, 0.25)
    norm_gain = jnp.clip(1.0 + 0.1 * jax.random.normal(seeds[7], (D,), jnp.float32), 0.5, 1.5)
    expand_weight = noise(seeds[8], (FF, D), D ** -0.5, 0.25, ((0, 4),))
    reduce_weight = noise(seeds[9], (FF, D), FF ** -0.5, 0.125, ((0, 4),))
    return dict(features=features, tile_pattern=tile_pattern, tile_source=tile_source, serve_list=serve_list, key_blocks=key_blocks, qkv_weight=qkv_weight, attn_weight=attn_weight, norm_gain=norm_gain, expand_weight=expand_weight, reduce_weight=reduce_weight)


def reference(features, tile_pattern, tile_source, serve_list, key_blocks, qkv_weight, attn_weight, norm_gain, expand_weight, reduce_weight):
    block_count = features.shape[0] // BLOCK
    blocks = features.reshape(block_count, BLOCK, D)
    block_ids = jnp.arange(block_count, dtype=jnp.int32)
    device_id = block_ids // BLK_DEV
    domain = (device_id // N_HEAD)[:, None]
    head_slot = (device_id % N_HEAD)[:, None]
    entries = tile_source
    remote_entry = jnp.maximum(entries - BLK_DEV, 0)
    peer_domain = remote_entry // SLOTS
    slot_index = remote_entry % SLOTS
    local_index = serve_list[peer_domain, head_slot, domain, slot_index]
    remote_block = (peer_domain * N_HEAD + head_slot) * BLK_DEV + local_index
    own_block = device_id[:, None] * BLK_DEV + entries
    source_block = jnp.where(entries < BLK_DEV, own_block, remote_block).astype(jnp.int32)

    def one_block(inputs):
        pattern_block, source_ids, own_rows = inputs
        sources = blocks[source_ids]
        summed = jnp.einsum('tij,tjf->if', pattern_block.astype(jnp.float32), sources.astype(jnp.float32))
        degree = lax.optimization_barrier(jnp.sum(pattern_block, axis=(0, 2))).astype(jnp.float32)
        return ((own_rows.astype(jnp.float32) + summed) * lax.rsqrt(1.0 + degree)[:, None]).astype(jnp.bfloat16)
    aggregated = lax.map(one_block, (tile_pattern, source_block, blocks)).reshape(-1, D)
    qkv = jnp.dot(aggregated, qkv_weight, preferred_element_type=jnp.float32).astype(jnp.bfloat16)
    qkv_parts = qkv.reshape(N_DOM, BLK_PART, BLOCK, HEADS, 3, HDIM)
    key_parts = key_blocks.reshape(N_DOM, BLK_PART, KB)
    score_scale = 1.0 / HDIM ** 0.5

    def one_part(inputs):
        part_qkv, part_keys = inputs

        def one_query(query_index):
            queries = part_qkv[query_index][:, :, 0, :].astype(jnp.float32)
            selected = part_qkv[part_keys[query_index]]
            keys = selected[:, :, :, 1, :].reshape(KB * BLOCK, HEADS, HDIM).astype(jnp.float32)
            values = selected[:, :, :, 2, :].reshape(KB * BLOCK, HEADS, HDIM).astype(jnp.float32)
            scores = jnp.einsum('qhe,khe->hqk', queries, keys) * score_scale
            row_max = lax.optimization_barrier(jnp.max(scores, axis=-1, keepdims=True))
            exp_terms = jnp.exp(scores - row_max)
            probabilities = (exp_terms / lax.optimization_barrier(jnp.sum(exp_terms, axis=-1, keepdims=True))).astype(jnp.bfloat16)
            context = jnp.einsum('hqk,khe->qhe', probabilities.astype(jnp.float32), values)
            return context.astype(jnp.bfloat16)
        return lax.map(one_query, jnp.arange(BLK_PART, dtype=jnp.int32))
    context = lax.map(one_part, (qkv_parts, key_parts)).reshape(-1, D)
    mixed = aggregated.astype(jnp.float32) + jnp.dot(context, attn_weight, preferred_element_type=jnp.float32)
    mean_square = lax.optimization_barrier(jnp.mean(mixed * mixed, axis=-1, keepdims=True))
    normed = (mixed * lax.rsqrt(mean_square + 1e-06) * norm_gain).astype(jnp.bfloat16)
    expanded = jnp.dot(normed, expand_weight.T, preferred_element_type=jnp.float32)
    hidden = jax.nn.gelu(expanded).astype(jnp.bfloat16)
    result = normed.astype(jnp.float32) + jnp.dot(hidden, reduce_weight, preferred_element_type=jnp.float32)
    return result.astype(jnp.bfloat16)
```

```python
import functools
import math

import jax
import jax.numpy as jnp
from jax import lax
from jax.experimental import pallas as pl
from jax.experimental.pallas import tpu as pltpu
from jax.sharding import PartitionSpec as P

HEADS = 16
HDIM = 32
LANES = 128
CHUNKS = 2
PER_GROUP = LANES // HDIM
GROUPS = HEADS // PER_GROUP
MESH = pl.DeviceIdType.MESH
F32 = jnp.float32
BF16 = jnp.bfloat16


def dot(a, b):
    return lax.dot_general(a, b, (((1,), (0,)), ((), ())), preferred_element_type=F32)


def dot_t(a, b):
    return lax.dot_general(a, b, (((1,), (1,)), ((), ())), preferred_element_type=F32)


def kernel(
    nd,
    nh,
    features,
    pattern_hbm,
    tile_source,
    serve,
    key_blocks,
    qkv_hbm,
    attn_hbm,
    gain,
    expand_hbm,
    reduce_hbm,
    out,
    *scratch,
):
    stage = scratch[:CHUNKS]
    table = scratch[CHUNKS : 2 * CHUNKS]
    gathered = scratch[2 * CHUNKS : 3 * CHUNKS]
    (
        pattern,
        pattern16,
        scale_rows,
        qkv_raw,
        weight_q,
        weight_kv,
        weight_o,
        expand,
        reduce_w,
        queries,
        context,
        normed,
        total,
        local_sem,
        dom_send,
        dom_recv,
        agg_send,
        agg_recv,
        w_send,
        w_recv,
        fwd_send,
        fwd_recv,
    ) = scratch[3 * CHUNKS :]
    d = lax.axis_index("dom")
    h = lax.axis_index("head")
    blk, tiles, rows, _ = pattern.shape
    width = features.shape[2]
    nodes = blk * rows
    cw = width // CHUNKS
    shard = expand_hbm.shape[0]
    half = shard // 2
    core = lax.rem(d, 2)
    sibling = d + 1 - 2 * core
    dom_peers = [lax.rem(d + k, nd) for k in range(1, nd)]
    head_peers = [lax.rem(h + k, nh) for k in range(1, nh)]

    barrier = pltpu.get_barrier_semaphore()
    for p in dom_peers:
        pl.semaphore_signal(barrier, inc=1, device_id=(p, h), device_id_type=MESH)
    for q in head_peers:
        pl.semaphore_signal(barrier, inc=1, device_id=(d, q), device_id_type=MESH)

    loads = [
        pltpu.make_async_copy(pattern_hbm, pattern, local_sem.at[0]),
        pltpu.make_async_copy(qkv_hbm, qkv_raw, local_sem.at[1]),
        pltpu.make_async_copy(attn_hbm, weight_o, local_sem.at[2]),
        pltpu.make_async_copy(expand_hbm, expand.at[pl.ds(h * shard, shard)], local_sem.at[3]),
        pltpu.make_async_copy(reduce_hbm, reduce_w.at[pl.ds(h * shard, shard)], local_sem.at[4]),
    ]
    for copy in loads:
        copy.start()

    for c in range(CHUNKS):
        for p in dom_peers:
            stage[c][p] = features[serve[0, 0, p, 0], :, c * cw : (c + 1) * cw]

    def dom_copy(c, to, slot, send, recv):
        return pltpu.make_async_remote_copy(
            src_ref=stage[c].at[to],
            dst_ref=table[c].at[blk + slot],
            send_sem=dom_send.at[c, send],
            recv_sem=dom_recv.at[c, recv],
            device_id=(to, h),
            device_id_type=MESH,
        )

    def agg_copy(c, to, owner):
        part = gathered[c].at[pl.ds(owner * blk, blk)]
        return pltpu.make_async_remote_copy(
            src_ref=part,
            dst_ref=part,
            send_sem=agg_send.at[c, to],
            recv_sem=agg_recv.at[c, owner],
            device_id=(d, to),
            device_id_type=MESH,
        )

    def weight_copy(which, to, owner):
        source = (expand_hbm, reduce_hbm)[which]
        target = (expand, reduce_w)[which]
        return pltpu.make_async_remote_copy(
            src_ref=source.at[pl.ds(core * half, half)],
            dst_ref=target.at[pl.ds(owner * shard + core * half, half)],
            send_sem=w_send.at[which, to],
            recv_sem=w_recv.at[which, owner],
            device_id=(d, to),
            device_id_type=MESH,
        )

    def forward_copy(which, owner, side):
        part = (expand, reduce_w)[which].at[pl.ds(owner * shard + side * half, half)]
        return pltpu.make_async_remote_copy(
            src_ref=part,
            dst_ref=part,
            send_sem=fwd_send.at[which, owner],
            recv_sem=fwd_recv.at[which, owner],
            device_id=(sibling, h),
            device_id_type=MESH,
        )

    pl.semaphore_wait(barrier, nd + nh - 2)
    for c in range(CHUNKS):
        for p in dom_peers:
            dom_copy(c, p, d, p, d).start()
    for which in range(2):
        for q in head_peers:
            weight_copy(which, q, h).start()

    for c in range(CHUNKS):
        for b in range(blk):
            table[c][b] = features[b, :, c * cw : (c + 1) * cw]
        table[c][blk + d] = features[serve[0, 0, d, 0], :, c * cw : (c + 1) * cw]

    loads[0].wait()
    for b in range(blk):
        tile_sum = pattern[b, 0]
        for t in range(tiles):
            tile = pattern[b, t]
            pattern16[b, :, t * rows : (t + 1) * rows] = tile.astype(F32).astype(BF16)
            if t:
                tile_sum = tile_sum + tile
        degree = jnp.sum(tile_sum.astype(F32), axis=1, keepdims=True)
        scale_rows[b] = jnp.broadcast_to(lax.rsqrt(1.0 + degree), (rows, LANES))

    loads[1].wait()
    span = 3 * LANES
    source_col = lax.broadcasted_iota(jnp.int32, (span, span), 0)
    target_col = lax.broadcasted_iota(jnp.int32, (span, span), 1)
    kind = target_col // LANES
    head = (target_col // HDIM) % PER_GROUP
    entry = target_col % HDIM
    reorder = (source_col == (3 * head + kind) * HDIM + entry).astype(F32).astype(BF16)
    for g in range(GROUPS):
        moved = dot(qkv_raw[:, g * span : (g + 1) * span], reorder).astype(BF16)
        lo = g * LANES
        weight_q[:, lo : lo + LANES] = moved[:, :LANES]
        weight_kv[:, lo : lo + LANES] = moved[:, LANES : 2 * LANES]
        weight_kv[:, width + lo : width + lo + LANES] = moved[:, 2 * LANES :]
    for copy in loads[2:]:
        copy.wait()

    for c in range(CHUNKS):
        for p in dom_peers:
            dom_copy(c, d, p, d, p).wait_recv()
        for b in range(blk):
            sources = jnp.concatenate([table[c][tile_source[b, t]] for t in range(tiles)], axis=0)
            summed = dot(pattern16[b], sources)
            own = features[b, :, c * cw : (c + 1) * cw].astype(F32)
            scaled = (own + summed) * scale_rows[b, :, 0:1]
            gathered[c][h * blk + b] = scaled.astype(BF16)
        for q in head_peers:
            agg_copy(c, q, h).start()

    own_rows = jnp.concatenate(
        [gathered[c][pl.ds(h * blk, blk)].reshape(nodes, cw) for c in range(CHUNKS)], axis=1
    )
    queries[...] = dot(own_rows, weight_q[...]).astype(BF16)

    for which in range(2):
        for q in head_peers:
            weight_copy(which, h, q).wait_recv()
            forward_copy(which, q, core).start()

    for c in range(CHUNKS):
        for q in head_peers:
            agg_copy(c, h, q).wait_recv()

    chosen = key_blocks.shape[1]
    lane_head = lax.broadcasted_iota(jnp.int32, (rows, LANES), 1) // HDIM
    factor = math.log2(math.e) / math.sqrt(HDIM)

    def attend(b, carry):
        ids = [key_blocks[h * blk + b, k] for k in range(chosen)]
        picked = jnp.concatenate(
            [
                jnp.concatenate([gathered[c][i] for c in range(CHUNKS)], axis=1)
                for i in ids
            ],
            axis=0,
        )
        pairs = dot(picked, weight_kv[...]).astype(BF16)
        at = pl.multiple_of(b * rows, rows)
        for g in range(GROUPS):
            lo = g * LANES
            query = queries[pl.ds(at, rows), lo : lo + LANES]
            zero = jnp.zeros_like(query)
            stacked = jnp.concatenate(
                [jnp.where(lane_head == a, query, zero) for a in range(PER_GROUP)], axis=0
            )
            scores = dot_t(stacked, pairs[:, lo : lo + LANES])
            row_max = jnp.max(scores, axis=1, keepdims=True)
            terms = jnp.exp2((scores - row_max) * factor)
            weights = terms * (1.0 / jnp.sum(terms, axis=1, keepdims=True))
            mixed_values = dot(weights.astype(BF16), pairs[:, width + lo : width + lo + LANES])
            merged = mixed_values[:rows]
            for a in range(1, PER_GROUP):
                merged = jnp.where(lane_head == a, mixed_values[a * rows : (a + 1) * rows], merged)
            context[pl.ds(at, rows), lo : lo + LANES] = merged.astype(BF16)
        return carry

    lax.fori_loop(0, blk, attend, 0)

    own_rows = jnp.concatenate(
        [gathered[c][pl.ds(h * blk, blk)].reshape(nodes, cw) for c in range(CHUNKS)], axis=1
    )
    mixed = own_rows.astype(F32) + dot(context[...], weight_o[...])
    mean_square = jnp.mean(mixed * mixed, axis=1, keepdims=True)
    normed[...] = (mixed * lax.rsqrt(mean_square + 1e-06) * gain[...]).astype(BF16)

    for which in range(2):
        for q in head_peers:
            forward_copy(which, q, 1 - core).wait_recv()

    total[...] = normed[...].astype(F32)
    step = 512

    def feed(i, carry):
        at = pl.multiple_of(i * step, step)
        expanded = dot_t(normed[...], expand[pl.ds(at, step)])
        activated = jax.nn.gelu(expanded).astype(BF16)
        total[...] += dot(activated, reduce_w[pl.ds(at, step)])
        return carry

    lax.fori_loop(0, nh * shard // step, feed, 0)
    out[...] = total[...].astype(BF16)

    for c in range(CHUNKS):
        for p in dom_peers:
            dom_copy(c, p, d, p, d).wait_send()
        for q in head_peers:
            agg_copy(c, q, h).wait_send()
    for which in range(2):
        for q in head_peers:
            weight_copy(which, q, h).wait_send()
            forward_copy(which, q, core).wait_send()


def solution(mesh):
    nd, nh = mesh.shape["dom"], mesh.shape["head"]

    def shards(
        features,
        tile_pattern,
        tile_source,
        serve_list,
        key_blocks,
        qkv_weight,
        attn_weight,
        norm_gain,
        expand_weight,
        reduce_weight,
    ):
        blk, tiles, rows, _ = tile_pattern.shape
        nodes, width = features.shape
        cw = width // CHUNKS
        ff = expand_weight.shape[0] * nh
        vmem = pl.BlockSpec(memory_space=pltpu.VMEM)
        smem = pl.BlockSpec(memory_space=pltpu.SMEM)
        hbm = pl.BlockSpec(memory_space=pl.ANY)
        scratch = (
            [pltpu.VMEM((nd, rows, cw), BF16) for _ in range(CHUNKS)]
            + [pltpu.VMEM((blk + nd, rows, cw), BF16) for _ in range(CHUNKS)]
            + [pltpu.VMEM((nh * blk, rows, cw), BF16) for _ in range(CHUNKS)]
            + [
                pltpu.VMEM(tile_pattern.shape, jnp.int32),
                pltpu.VMEM((blk, rows, tiles * rows), BF16),
                pltpu.VMEM((blk, rows, LANES), F32),
                pltpu.VMEM(qkv_weight.shape, BF16),
                pltpu.VMEM((width, width), BF16),
                pltpu.VMEM((width, 2 * width), BF16),
                pltpu.VMEM(attn_weight.shape, BF16),
                pltpu.VMEM((ff, width), BF16),
                pltpu.VMEM((ff, width), BF16),
                pltpu.VMEM((nodes, width), BF16),
                pltpu.VMEM((nodes, width), BF16),
                pltpu.VMEM((nodes, width), BF16),
                pltpu.VMEM((nodes, width), F32),
                pltpu.SemaphoreType.DMA((5,)),
                pltpu.SemaphoreType.DMA((CHUNKS, nd)),
                pltpu.SemaphoreType.DMA((CHUNKS, nd)),
                pltpu.SemaphoreType.DMA((CHUNKS, nh)),
                pltpu.SemaphoreType.DMA((CHUNKS, nh)),
                pltpu.SemaphoreType.DMA((2, nh)),
                pltpu.SemaphoreType.DMA((2, nh)),
                pltpu.SemaphoreType.DMA((2, nh)),
                pltpu.SemaphoreType.DMA((2, nh)),
            ]
        )
        return pl.pallas_call(
            functools.partial(kernel, nd, nh),
            out_shape=jax.ShapeDtypeStruct((nodes, width), BF16),
            in_specs=[vmem, hbm, smem, smem, smem, hbm, hbm, vmem, hbm, hbm],
            out_specs=vmem,
            scratch_shapes=scratch,
            compiler_params=pltpu.CompilerParams(
                collective_id=0, has_side_effects=True, vmem_limit_bytes=56 * 1024 * 1024
            ),
        )(
            features.reshape(blk, rows, width),
            tile_pattern,
            tile_source,
            serve_list,
            key_blocks,
            qkv_weight,
            attn_weight,
            norm_gain.reshape(1, -1),
            expand_weight,
            reduce_weight,
        )

    placed = (
        P(("dom", "head"), None),
        P(("dom", "head"), None, None, None),
        P(("dom", "head"), None),
        P("dom", "head", None, None),
        P("dom", None),
        P(),
        P(),
        P(),
        P("head", None),
        P("head", None),
    )
    return jax.shard_map(
        shards, mesh=mesh, in_specs=placed, out_specs=P(("dom", "head"), None), check_vma=False
    )
```

```python
import functools
import math

import jax
import jax.numpy as jnp
from jax import lax
from jax.experimental import pallas as pl
from jax.experimental.pallas import tpu as pltpu
from jax.sharding import PartitionSpec as P

HEADS = 16
HDIM = 32
LANES = 128
CHUNKS = 4
DEPTH = 2
PER_GROUP = LANES // HDIM
GROUPS = HEADS // PER_GROUP
FETCH_STEP = 1
MESH = pl.DeviceIdType.MESH
F32 = jnp.float32
BF16 = jnp.bfloat16


def dot(a, b):
    return lax.dot_general(a, b, (((1,), (0,)), ((), ())), preferred_element_type=F32)


def dot_t(a, b):
    return lax.dot_general(a, b, (((1,), (1,)), ((), ())), preferred_element_type=F32)


def kernel(
    nd,
    nh,
    features,
    pattern_hbm,
    tile_source,
    serve,
    key_blocks,
    qkv_hbm,
    attn_hbm,
    gain,
    expand_hbm,
    reduce_hbm,
    out,
    *scratch,
):
    stage = scratch[:CHUNKS]
    table = scratch[CHUNKS : 2 * CHUNKS]
    gathered = scratch[2 * CHUNKS : 3 * CHUNKS]
    (
        pattern,
        pattern16,
        scale_rows,
        qkv_raw,
        weight_q,
        weight_kv,
        weight_o,
        expand,
        reduce_w,
        queries,
        context,
        normed,
        total,
        local_sem,
        dom_send,
        dom_recv,
        agg_send,
        agg_recv,
        w_send,
        w_recv,
        pair_send,
        pair_recv,
        fwd_send,
        fwd_recv,
    ) = scratch[3 * CHUNKS :]
    d = lax.axis_index("dom")
    h = lax.axis_index("head")
    blk, tiles, rows, _ = pattern.shape
    width = features.shape[2]
    nodes = blk * rows
    cw = width // CHUNKS
    shard = expand_hbm.shape[0]
    half = shard // 2
    quarter = shard // 4
    core = lax.rem(d, 2)
    sibling = d + 1 - 2 * core
    pair = lax.rem(d // 2, 2)
    partner = d + 2 - 4 * pair
    dom_peers = [lax.rem(d + k, nd) for k in range(1, nd)]
    head_peers = [lax.rem(h + k, nh) for k in range(1, nh)]

    barrier = pltpu.get_barrier_semaphore()
    for p in dom_peers:
        pl.semaphore_signal(barrier, inc=1, device_id=(p, h), device_id_type=MESH)
    for q in head_peers:
        pl.semaphore_signal(barrier, inc=1, device_id=(d, q), device_id_type=MESH)

    loads = [
        pltpu.make_async_copy(pattern_hbm, pattern, local_sem.at[0]),
        pltpu.make_async_copy(qkv_hbm, qkv_raw, local_sem.at[1]),
        pltpu.make_async_copy(attn_hbm, weight_o, local_sem.at[2]),
        pltpu.make_async_copy(expand_hbm, expand.at[pl.ds(h * shard, shard)], local_sem.at[3]),
        pltpu.make_async_copy(reduce_hbm, reduce_w.at[pl.ds(h * shard, shard)], local_sem.at[4]),
    ]
    for copy in loads:
        copy.start()

    for c in range(CHUNKS):
        for p in dom_peers:
            stage[c][p] = features[serve[0, 0, p, 0], :, c * cw : (c + 1) * cw]

    def dom_copy(c, to, slot, send, recv):
        return pltpu.make_async_remote_copy(
            src_ref=stage[c].at[to],
            dst_ref=table[c].at[blk + slot],
            send_sem=dom_send.at[c, send],
            recv_sem=dom_recv.at[c, recv],
            device_id=(to, h),
            device_id_type=MESH,
        )

    def agg_copy(c, to, owner):
        part = gathered[c].at[pl.ds(owner * blk, blk)]
        return pltpu.make_async_remote_copy(
            src_ref=part,
            dst_ref=part,
            send_sem=agg_send.at[c, to],
            recv_sem=agg_recv.at[c, owner],
            device_id=(d, to),
            device_id_type=MESH,
        )

    def weight_copy(which, to, owner):
        source = (expand_hbm, reduce_hbm)[which]
        target = (expand, reduce_w)[which]
        return pltpu.make_async_remote_copy(
            src_ref=source.at[pl.ds(core * half + pair * quarter, quarter)],
            dst_ref=target.at[pl.ds(owner * shard + core * half + pair * quarter, quarter)],
            send_sem=w_send.at[which, to],
            recv_sem=w_recv.at[which, owner],
            device_id=(d, to),
            device_id_type=MESH,
        )

    def pair_copy(which, owner, side):
        at = owner * shard + core * half + side * quarter
        part = (expand, reduce_w)[which].at[pl.ds(at, quarter)]
        return pltpu.make_async_remote_copy(
            src_ref=part,
            dst_ref=part,
            send_sem=pair_send.at[which, owner],
            recv_sem=pair_recv.at[which, owner],
            device_id=(partner, h),
            device_id_type=MESH,
        )

    def forward_copy(which, owner, side):
        part = (expand, reduce_w)[which].at[pl.ds(owner * shard + side * half, half)]
        return pltpu.make_async_remote_copy(
            src_ref=part,
            dst_ref=part,
            send_sem=fwd_send.at[which, owner],
            recv_sem=fwd_recv.at[which, owner],
            device_id=(sibling, h),
            device_id_type=MESH,
        )

    pl.semaphore_wait(barrier, nd + nh - 2)
    for c in range(DEPTH):
        for p in dom_peers:
            dom_copy(c, p, d, p, d).start()
    for which in range(2):
        for q in head_peers:
            weight_copy(which, q, h).start()

    for c in range(CHUNKS):
        for b in range(blk):
            table[c][b] = features[b, :, c * cw : (c + 1) * cw]
        table[c][blk + d] = features[serve[0, 0, d, 0], :, c * cw : (c + 1) * cw]

    loads[0].wait()
    for b in range(blk):
        tile_sum = pattern[b, 0]
        for t in range(tiles):
            tile = pattern[b, t]
            pattern16[b, :, t * rows : (t + 1) * rows] = tile.astype(F32).astype(BF16)
            if t:
                tile_sum = tile_sum + tile
        degree = jnp.sum(tile_sum.astype(F32), axis=1, keepdims=True)
        scale_rows[b] = jnp.broadcast_to(lax.rsqrt(1.0 + degree), (rows, LANES))

    loads[1].wait()
    span = 3 * LANES
    source_col = lax.broadcasted_iota(jnp.int32, (span, span), 0)
    target_col = lax.broadcasted_iota(jnp.int32, (span, span), 1)
    kind = target_col // LANES
    head = (target_col // HDIM) % PER_GROUP
    entry = target_col % HDIM
    reorder = (source_col == (3 * head + kind) * HDIM + entry).astype(F32).astype(BF16)
    for g in range(GROUPS):
        moved = dot(qkv_raw[:, g * span : (g + 1) * span], reorder).astype(BF16)
        lo = g * LANES
        weight_q[:, lo : lo + LANES] = moved[:, :LANES]
        weight_kv[:, lo : lo + LANES] = moved[:, LANES : 2 * LANES]
        weight_kv[:, width + lo : width + lo + LANES] = moved[:, 2 * LANES :]
    for copy in loads[2:]:
        copy.wait()

    for c in range(CHUNKS):
        for p in dom_peers:
            dom_copy(c, d, p, d, p).wait_recv()
        if c + DEPTH < CHUNKS:
            for p in dom_peers:
                dom_copy(c + DEPTH, p, d, p, d).start()
        for b in range(blk):
            sources = jnp.concatenate([table[c][tile_source[b, t]] for t in range(tiles)], axis=0)
            summed = dot(pattern16[b], sources)
            own = features[b, :, c * cw : (c + 1) * cw].astype(F32)
            scaled = (own + summed) * scale_rows[b, :, 0:1]
            gathered[c][h * blk + b] = scaled.astype(BF16)
        for q in head_peers:
            agg_copy(c, q, h).start()
        if c == FETCH_STEP:
            for which in range(2):
                for q in head_peers:
                    weight_copy(which, h, q).wait_recv()
                    pair_copy(which, q, pair).start()

    own_rows = jnp.concatenate(
        [gathered[c][pl.ds(h * blk, blk)].reshape(nodes, cw) for c in range(CHUNKS)], axis=1
    )
    queries[...] = dot(own_rows, weight_q[...]).astype(BF16)

    for c in range(CHUNKS):
        for q in head_peers:
            agg_copy(c, h, q).wait_recv()

    for which in range(2):
        for q in head_peers:
            pair_copy(which, q, 1 - pair).wait_recv()
            forward_copy(which, q, core).start()

    chosen = key_blocks.shape[1]
    lane_head = lax.broadcasted_iota(jnp.int32, (rows, LANES), 1) // HDIM
    factor = math.log2(math.e) / math.sqrt(HDIM)

    def attend(b, carry):
        ids = [key_blocks[h * blk + b, k] for k in range(chosen)]
        picked = jnp.concatenate(
            [
                jnp.concatenate([gathered[c][i] for c in range(CHUNKS)], axis=1)
                for i in ids
            ],
            axis=0,
        )
        pairs = dot(picked, weight_kv[...]).astype(BF16)
        at = pl.multiple_of(b * rows, rows)
        for g in range(GROUPS):
            lo = g * LANES
            query = queries[pl.ds(at, rows), lo : lo + LANES]
            zero = jnp.zeros_like(query)
            stacked = jnp.concatenate(
                [jnp.where(lane_head == a, query, zero) for a in range(PER_GROUP)], axis=0
            )
            scores = dot_t(stacked, pairs[:, lo : lo + LANES])
            row_max = jnp.max(scores, axis=1, keepdims=True)
            terms = jnp.exp2((scores - row_max) * factor)
            weights = terms * (1.0 / jnp.sum(terms, axis=1, keepdims=True))
            mixed_values = dot(weights.astype(BF16), pairs[:, width + lo : width + lo + LANES])
            merged = mixed_values[:rows]
            for a in range(1, PER_GROUP):
                merged = jnp.where(lane_head == a, mixed_values[a * rows : (a + 1) * rows], merged)
            context[pl.ds(at, rows), lo : lo + LANES] = merged.astype(BF16)
        return carry

    lax.fori_loop(0, blk, attend, 0, unroll=True)


    own_rows = jnp.concatenate(
        [gathered[c][pl.ds(h * blk, blk)].reshape(nodes, cw) for c in range(CHUNKS)], axis=1
    )
    mixed = own_rows.astype(F32) + dot(context[...], weight_o[...])
    mean_square = jnp.mean(mixed * mixed, axis=1, keepdims=True)
    normed[...] = (mixed * lax.rsqrt(mean_square + 1e-06) * gain[...]).astype(BF16)

    for which in range(2):
        for q in head_peers:
            forward_copy(which, q, 1 - core).wait_recv()

    total[...] = normed[...].astype(F32)
    step = 512

    def feed(i, carry):
        at = pl.multiple_of(i * step, step)
        expanded = dot_t(normed[...], expand[pl.ds(at, step)])
        activated = jax.nn.gelu(expanded).astype(BF16)
        total[...] += dot(activated, reduce_w[pl.ds(at, step)])
        return carry

    lax.fori_loop(0, nh * shard // step, feed, 0, unroll=True)
    out[...] = total[...].astype(BF16)

    for c in range(CHUNKS):
        for p in dom_peers:
            dom_copy(c, p, d, p, d).wait_send()
        for q in head_peers:
            agg_copy(c, q, h).wait_send()
    for which in range(2):
        for q in head_peers:
            weight_copy(which, q, h).wait_send()
            pair_copy(which, q, pair).wait_send()
            forward_copy(which, q, core).wait_send()


def solution(mesh):
    nd, nh = mesh.shape["dom"], mesh.shape["head"]

    def shards(
        features,
        tile_pattern,
        tile_source,
        serve_list,
        key_blocks,
        qkv_weight,
        attn_weight,
        norm_gain,
        expand_weight,
        reduce_weight,
    ):
        blk, tiles, rows, _ = tile_pattern.shape
        nodes, width = features.shape
        cw = width // CHUNKS
        ff = expand_weight.shape[0] * nh
        vmem = pl.BlockSpec(memory_space=pltpu.VMEM)
        smem = pl.BlockSpec(memory_space=pltpu.SMEM)
        hbm = pl.BlockSpec(memory_space=pl.ANY)
        scratch = (
            [pltpu.VMEM((nd, rows, cw), BF16) for _ in range(CHUNKS)]
            + [pltpu.VMEM((blk + nd, rows, cw), BF16) for _ in range(CHUNKS)]
            + [pltpu.VMEM((nh * blk, rows, cw), BF16) for _ in range(CHUNKS)]
            + [
                pltpu.VMEM(tile_pattern.shape, jnp.int32),
                pltpu.VMEM((blk, rows, tiles * rows), BF16),
                pltpu.VMEM((blk, rows, LANES), F32),
                pltpu.VMEM(qkv_weight.shape, BF16),
                pltpu.VMEM((width, width), BF16),
                pltpu.VMEM((width, 2 * width), BF16),
                pltpu.VMEM(attn_weight.shape, BF16),
                pltpu.VMEM((ff, width), BF16),
                pltpu.VMEM((ff, width), BF16),
                pltpu.VMEM((nodes, width), BF16),
                pltpu.VMEM((nodes, width), BF16),
                pltpu.VMEM((nodes, width), BF16),
                pltpu.VMEM((nodes, width), F32),
                pltpu.SemaphoreType.DMA((5,)),
                pltpu.SemaphoreType.DMA((CHUNKS, nd)),
                pltpu.SemaphoreType.DMA((CHUNKS, nd)),
                pltpu.SemaphoreType.DMA((CHUNKS, nh)),
                pltpu.SemaphoreType.DMA((CHUNKS, nh)),
                pltpu.SemaphoreType.DMA((2, nh)),
                pltpu.SemaphoreType.DMA((2, nh)),
                pltpu.SemaphoreType.DMA((2, nh)),
                pltpu.SemaphoreType.DMA((2, nh)),
                pltpu.SemaphoreType.DMA((2, nh)),
                pltpu.SemaphoreType.DMA((2, nh)),
            ]
        )
        return pl.pallas_call(
            functools.partial(kernel, nd, nh),
            out_shape=jax.ShapeDtypeStruct((nodes, width), BF16),
            in_specs=[vmem, hbm, smem, smem, smem, hbm, hbm, vmem, hbm, hbm],
            out_specs=vmem,
            scratch_shapes=scratch,
            compiler_params=pltpu.CompilerParams(
                collective_id=0, has_side_effects=True, vmem_limit_bytes=56 * 1024 * 1024
            ),
        )(
            features.reshape(blk, rows, width),
            tile_pattern,
            tile_source,
            serve_list,
            key_blocks,
            qkv_weight,
            attn_weight,
            norm_gain.reshape(1, -1),
            expand_weight,
            reduce_weight,
        )

    placed = (
        P(("dom", "head"), None),
        P(("dom", "head"), None, None, None),
        P(("dom", "head"), None),
        P("dom", "head", None, None),
        P("dom", None),
        P(),
        P(),
        P(),
        P("head", None),
        P("head", None),
    )
    return jax.shard_map(
        shards, mesh=mesh, in_specs=placed, out_specs=P(("dom", "head"), None), check_vma=False
    )
```

```python
import functools
import math

import jax
import jax.numpy as jnp
from jax import lax
from jax.experimental import pallas as pl
from jax.experimental.pallas import tpu as pltpu
from jax.sharding import PartitionSpec as P

HEADS = 16
HDIM = 32
LANES = 128
CHUNKS = 4
DEPTH = 2
PER_GROUP = LANES // HDIM
GROUPS = HEADS // PER_GROUP
FETCH_STEP = 1
MESH = pl.DeviceIdType.MESH
F32 = jnp.float32
BF16 = jnp.bfloat16


def dot(a, b):
    return lax.dot_general(a, b, (((1,), (0,)), ((), ())), preferred_element_type=F32)


def dot_t(a, b):
    return lax.dot_general(a, b, (((1,), (1,)), ((), ())), preferred_element_type=F32)


def kernel(
    nd,
    nh,
    features,
    pattern_hbm,
    tile_source,
    serve,
    key_blocks,
    qkv_hbm,
    attn_hbm,
    gain,
    expand_hbm,
    reduce_hbm,
    out,
    *scratch,
):
    stage = scratch[:CHUNKS]
    table = scratch[CHUNKS : 2 * CHUNKS]
    gathered = scratch[2 * CHUNKS : 3 * CHUNKS]
    (
        pattern,
        pattern16,
        scale_rows,
        qkv_raw,
        weight_q,
        weight_kv,
        weight_o,
        expand,
        reduce_w,
        queries,
        context,
        normed,
        total,
        local_sem,
        dom_send,
        dom_recv,
        agg_send,
        agg_recv,
        w_send,
        w_recv,
        pair_send,
        pair_recv,
        fwd_send,
        fwd_recv,
    ) = scratch[3 * CHUNKS :]
    d = lax.axis_index("dom")
    h = lax.axis_index("head")
    blk, tiles, rows, _ = pattern.shape
    width = features.shape[2]
    nodes = blk * rows
    cw = width // CHUNKS
    shard = expand_hbm.shape[0]
    half = shard // 2
    quarter = shard // 4
    core = lax.rem(d, 2)
    sibling = d + 1 - 2 * core
    pair = lax.rem(d // 2, 2)
    partner = d + 2 - 4 * pair
    dom_peers = [lax.rem(d + k, nd) for k in range(1, nd)]
    head_peers = [lax.rem(h + k, nh) for k in range(1, nh)]

    barrier = pltpu.get_barrier_semaphore()
    for p in dom_peers:
        pl.semaphore_signal(barrier, inc=1, device_id=(p, h), device_id_type=MESH)
    for q in head_peers:
        pl.semaphore_signal(barrier, inc=1, device_id=(d, q), device_id_type=MESH)

    loads = [
        pltpu.make_async_copy(pattern_hbm, pattern, local_sem.at[0]),
        pltpu.make_async_copy(qkv_hbm, qkv_raw, local_sem.at[1]),
        pltpu.make_async_copy(attn_hbm, weight_o, local_sem.at[2]),
        pltpu.make_async_copy(expand_hbm, expand.at[pl.ds(h * shard, shard)], local_sem.at[3]),
        pltpu.make_async_copy(reduce_hbm, reduce_w.at[pl.ds(h * shard, shard)], local_sem.at[4]),
    ]
    for copy in loads:
        copy.start()

    for c in range(CHUNKS):
        for p in dom_peers:
            stage[c][p] = features[serve[0, 0, p, 0], :, c * cw : (c + 1) * cw]

    def dom_copy(c, to, slot, send, recv):
        return pltpu.make_async_remote_copy(
            src_ref=stage[c].at[to],
            dst_ref=table[c].at[blk + slot],
            send_sem=dom_send.at[c, send],
            recv_sem=dom_recv.at[c, recv],
            device_id=(to, h),
            device_id_type=MESH,
        )

    def agg_copy(c, to, owner):
        part = gathered[c].at[pl.ds(owner * blk, blk)]
        return pltpu.make_async_remote_copy(
            src_ref=part,
            dst_ref=part,
            send_sem=agg_send.at[c, to],
            recv_sem=agg_recv.at[c, owner],
            device_id=(d, to),
            device_id_type=MESH,
        )

    def weight_copy(which, to, owner):
        source = (expand_hbm, reduce_hbm)[which]
        target = (expand, reduce_w)[which]
        return pltpu.make_async_remote_copy(
            src_ref=source.at[pl.ds(core * half + pair * quarter, quarter)],
            dst_ref=target.at[pl.ds(owner * shard + core * half + pair * quarter, quarter)],
            send_sem=w_send.at[which, to],
            recv_sem=w_recv.at[which, owner],
            device_id=(d, to),
            device_id_type=MESH,
        )

    def pair_copy(which, owner, side):
        at = owner * shard + core * half + side * quarter
        part = (expand, reduce_w)[which].at[pl.ds(at, quarter)]
        return pltpu.make_async_remote_copy(
            src_ref=part,
            dst_ref=part,
            send_sem=pair_send.at[which, owner],
            recv_sem=pair_recv.at[which, owner],
            device_id=(partner, h),
            device_id_type=MESH,
        )

    def forward_copy(which, owner, side):
        part = (expand, reduce_w)[which].at[pl.ds(owner * shard + side * half, half)]
        return pltpu.make_async_remote_copy(
            src_ref=part,
            dst_ref=part,
            send_sem=fwd_send.at[which, owner],
            recv_sem=fwd_recv.at[which, owner],
            device_id=(sibling, h),
            device_id_type=MESH,
        )

    pl.semaphore_wait(barrier, nd + nh - 2)
    for c in range(DEPTH):
        for p in dom_peers:
            dom_copy(c, p, d, p, d).start()
    for which in range(2):
        for q in head_peers:
            weight_copy(which, q, h).start()

    for c in range(CHUNKS):
        for b in range(blk):
            table[c][b] = features[b, :, c * cw : (c + 1) * cw]
        table[c][blk + d] = features[serve[0, 0, d, 0], :, c * cw : (c + 1) * cw]

    loads[0].wait()
    for b in range(blk):
        tile_sum = pattern[b, 0]
        for t in range(tiles):
            tile = pattern[b, t]
            pattern16[b, :, t * rows : (t + 1) * rows] = tile.astype(F32).astype(BF16)
            if t:
                tile_sum = tile_sum + tile
        degree = jnp.sum(tile_sum.astype(F32), axis=1, keepdims=True)
        scale_rows[b] = jnp.broadcast_to(lax.rsqrt(1.0 + degree), (rows, LANES))

    loads[1].wait()
    span = 3 * LANES
    source_col = lax.broadcasted_iota(jnp.int32, (span, span), 0)
    target_col = lax.broadcasted_iota(jnp.int32, (span, span), 1)
    kind = target_col // LANES
    head = (target_col // HDIM) % PER_GROUP
    entry = target_col % HDIM
    reorder = (source_col == (3 * head + kind) * HDIM + entry).astype(F32).astype(BF16)
    for g in range(GROUPS):
        moved = dot(qkv_raw[:, g * span : (g + 1) * span], reorder).astype(BF16)
        lo = g * LANES
        weight_q[:, lo : lo + LANES] = moved[:, :LANES]
        weight_kv[:, lo : lo + LANES] = moved[:, LANES : 2 * LANES]
        weight_kv[:, width + lo : width + lo + LANES] = moved[:, 2 * LANES :]
    for copy in loads[2:]:
        copy.wait()

    for c in range(CHUNKS):
        for p in dom_peers:
            dom_copy(c, d, p, d, p).wait_recv()
        if c + DEPTH < CHUNKS:
            for p in dom_peers:
                dom_copy(c + DEPTH, p, d, p, d).start()
        for b in range(blk):
            sources = jnp.concatenate([table[c][tile_source[b, t]] for t in range(tiles)], axis=0)
            summed = dot(pattern16[b], sources)
            own = features[b, :, c * cw : (c + 1) * cw].astype(F32)
            scaled = (own + summed) * scale_rows[b, :, 0:1]
            gathered[c][h * blk + b] = scaled.astype(BF16)
        for q in head_peers:
            agg_copy(c, q, h).start()
        if c == FETCH_STEP:
            for which in range(2):
                for q in head_peers:
                    weight_copy(which, h, q).wait_recv()
                    pair_copy(which, q, pair).start()

    own_rows = jnp.concatenate(
        [gathered[c][pl.ds(h * blk, blk)].reshape(nodes, cw) for c in range(CHUNKS)], axis=1
    )
    queries[...] = dot(own_rows, weight_q[...]).astype(BF16)

    for c in range(CHUNKS):
        for q in head_peers:
            agg_copy(c, h, q).wait_recv()

    chosen = key_blocks.shape[1]
    lane_head = lax.broadcasted_iota(jnp.int32, (rows, LANES), 1) // HDIM
    factor = math.log2(math.e) / math.sqrt(HDIM)

    def attend(b, carry):
        ids = [key_blocks[h * blk + b, k] for k in range(chosen)]
        picked = jnp.concatenate(
            [
                jnp.concatenate([gathered[c][i] for c in range(CHUNKS)], axis=1)
                for i in ids
            ],
            axis=0,
        )
        pairs = dot(picked, weight_kv[...]).astype(BF16)
        at = pl.multiple_of(b * rows, rows)
        for g in range(GROUPS):
            lo = g * LANES
            query = queries[pl.ds(at, rows), lo : lo + LANES]
            zero = jnp.zeros_like(query)
            stacked = jnp.concatenate(
                [jnp.where(lane_head == a, query, zero) for a in range(PER_GROUP)], axis=0
            )
            scores = dot_t(stacked, pairs[:, lo : lo + LANES])
            row_max = jnp.max(scores, axis=1, keepdims=True)
            terms = jnp.exp2((scores - row_max) * factor)
            weights = terms * (1.0 / jnp.sum(terms, axis=1, keepdims=True))
            mixed_values = dot(weights.astype(BF16), pairs[:, width + lo : width + lo + LANES])
            merged = mixed_values[:rows]
            for a in range(1, PER_GROUP):
                merged = jnp.where(lane_head == a, mixed_values[a * rows : (a + 1) * rows], merged)
            context[pl.ds(at, rows), lo : lo + LANES] = merged.astype(BF16)
        return carry

    early = blk // 2
    lax.fori_loop(0, early, attend, 0, unroll=True)

    for which in range(2):
        for q in head_peers:
            pair_copy(which, q, 1 - pair).wait_recv()
            forward_copy(which, q, core).start()

    lax.fori_loop(early, blk, attend, 0, unroll=True)


    own_rows = jnp.concatenate(
        [gathered[c][pl.ds(h * blk, blk)].reshape(nodes, cw) for c in range(CHUNKS)], axis=1
    )
    mixed = own_rows.astype(F32) + dot(context[...], weight_o[...])
    mean_square = jnp.mean(mixed * mixed, axis=1, keepdims=True)
    normed[...] = (mixed * lax.rsqrt(mean_square + 1e-06) * gain[...]).astype(BF16)

    total[...] = normed[...].astype(F32)
    for q in [h] + head_peers:
        if q is not h:
            for which in range(2):
                forward_copy(which, q, 1 - core).wait_recv()
        at = pl.multiple_of(q * shard, shard)
        expanded = dot_t(normed[...], expand[pl.ds(at, shard)])
        activated = jax.nn.gelu(expanded).astype(BF16)
        total[...] += dot(activated, reduce_w[pl.ds(at, shard)])
    out[...] = total[...].astype(BF16)

    for c in range(CHUNKS):
        for p in dom_peers:
            dom_copy(c, p, d, p, d).wait_send()
        for q in head_peers:
            agg_copy(c, q, h).wait_send()
    for which in range(2):
        for q in head_peers:
            weight_copy(which, q, h).wait_send()
            pair_copy(which, q, pair).wait_send()
            forward_copy(which, q, core).wait_send()


def solution(mesh):
    nd, nh = mesh.shape["dom"], mesh.shape["head"]

    def shards(
        features,
        tile_pattern,
        tile_source,
        serve_list,
        key_blocks,
        qkv_weight,
        attn_weight,
        norm_gain,
        expand_weight,
        reduce_weight,
    ):
        blk, tiles, rows, _ = tile_pattern.shape
        nodes, width = features.shape
        cw = width // CHUNKS
        ff = expand_weight.shape[0] * nh
        vmem = pl.BlockSpec(memory_space=pltpu.VMEM)
        smem = pl.BlockSpec(memory_space=pltpu.SMEM)
        hbm = pl.BlockSpec(memory_space=pl.ANY)
        scratch = (
            [pltpu.VMEM((nd, rows, cw), BF16) for _ in range(CHUNKS)]
            + [pltpu.VMEM((blk + nd, rows, cw), BF16) for _ in range(CHUNKS)]
            + [pltpu.VMEM((nh * blk, rows, cw), BF16) for _ in range(CHUNKS)]
            + [
                pltpu.VMEM(tile_pattern.shape, jnp.int32),
                pltpu.VMEM((blk, rows, tiles * rows), BF16),
                pltpu.VMEM((blk, rows, LANES), F32),
                pltpu.VMEM(qkv_weight.shape, BF16),
                pltpu.VMEM((width, width), BF16),
                pltpu.VMEM((width, 2 * width), BF16),
                pltpu.VMEM(attn_weight.shape, BF16),
                pltpu.VMEM((ff, width), BF16),
                pltpu.VMEM((ff, width), BF16),
                pltpu.VMEM((nodes, width), BF16),
                pltpu.VMEM((nodes, width), BF16),
                pltpu.VMEM((nodes, width), BF16),
                pltpu.VMEM((nodes, width), F32),
                pltpu.SemaphoreType.DMA((5,)),
                pltpu.SemaphoreType.DMA((CHUNKS, nd)),
                pltpu.SemaphoreType.DMA((CHUNKS, nd)),
                pltpu.SemaphoreType.DMA((CHUNKS, nh)),
                pltpu.SemaphoreType.DMA((CHUNKS, nh)),
                pltpu.SemaphoreType.DMA((2, nh)),
                pltpu.SemaphoreType.DMA((2, nh)),
                pltpu.SemaphoreType.DMA((2, nh)),
                pltpu.SemaphoreType.DMA((2, nh)),
                pltpu.SemaphoreType.DMA((2, nh)),
                pltpu.SemaphoreType.DMA((2, nh)),
            ]
        )
        return pl.pallas_call(
            functools.partial(kernel, nd, nh),
            out_shape=jax.ShapeDtypeStruct((nodes, width), BF16),
            in_specs=[vmem, hbm, smem, smem, smem, hbm, hbm, vmem, hbm, hbm],
            out_specs=vmem,
            scratch_shapes=scratch,
            compiler_params=pltpu.CompilerParams(
                collective_id=0, has_side_effects=True, vmem_limit_bytes=56 * 1024 * 1024
            ),
        )(
            features.reshape(blk, rows, width),
            tile_pattern,
            tile_source,
            serve_list,
            key_blocks,
            qkv_weight,
            attn_weight,
            norm_gain.reshape(1, -1),
            expand_weight,
            reduce_weight,
        )

    placed = (
        P(("dom", "head"), None),
        P(("dom", "head"), None, None, None),
        P(("dom", "head"), None),
        P("dom", "head", None, None),
        P("dom", None),
        P(),
        P(),
        P(),
        P("head", None),
        P("head", None),
    )
    return jax.shard_map(
        shards, mesh=mesh, in_specs=placed, out_specs=P(("dom", "head"), None), check_vma=False
    )
```
